256 devices in a mesh: row: 32 (over y, x, core), col: 8 (over z).
Axes of the slice: x: 4, y: 4, z: 8, core: 2. Of those that a mesh axis runs over, the one named last changes fastest.
Arguments:
- inputs: bfloat16 [4096, 8192], P('row'), may hold values from -1 to 1
- up_codes: int32 [8192, 14336], P('row', 'col'), may hold values from -128 to 127, as said below
- up_scales: float32 [64, 14336], P('row', 'col'), may hold values from 8e-05 to 0.0008
- gate_codes: int32 [8192, 14336], P('row', 'col'), may hold values from -128 to 127, as said below
- gate_scales: float32 [64, 14336], P('row', 'col'), may hold values from 8e-05 to 0.0008
- grad_up: bfloat16 [4096, 14336], P('row', 'col'), may hold values from -1 to 1
- grad_gate: bfloat16 [4096, 14336], P('row', 'col'), may hold values from -1 to 1
Outputs:
- input_grad: bfloat16 [4096, 8192], P('col', 'row')
- up_weight_grad: float32 [8192, 14336], P('row', 'col')
- gate_weight_grad: float32 [8192, 14336], P('row', 'col')
- up_scale_grad: float32 [64, 14336], P('row', 'col')
- gate_scale_grad: float32 [64, 14336], P('row', 'col')
The draws below stay inside these ranges and needn't reach their ends.
Inputs may be any that keep to these rules, and one draw needn't show every extreme that they name: `up_codes`: integer codes of int8 range held in int32; a share of them sits at each clip end. `gate_codes`: integer codes of int8 range held in int32; a share of them sits at each clip end.
All inputs are finite; a program needn't handle non-finite values.
Results may differ from the reference program's by a relative error of at most 0.017.
Values may be sent and summed in bfloat16 or wider, within the bound.
A program may use at most 128 MiB of HBM per device.

```python
import math
import jax
import jax.numpy as jnp
from jax import lax

D = 8192
F = 14336
GROUP = 128
TOKENS = 4096
N_COL = 8


def draw_up_codes(key, part):
    key = jax.random.fold_in(key, 11)
    raw = jax.random.randint(key, (D, F), -176, 176, dtype=jnp.int32)
    return jnp.clip(raw, -128, 127).astype(jnp.int32)


def draw_gate_codes(key, part):
    key = jax.random.fold_in(key, 23)
    raw = jax.random.randint(key, (D, F), -176, 176, dtype=jnp.int32)
    return jnp.clip(raw, -128, 127).astype(jnp.int32)


def block_levels(key, dims, split, least, largest):
    level, own = 1.0, jax.random.fold_in(key, 6)
    for position, shards_of in split:
        steps = jnp.exp(jax.random.uniform(jax.random.fold_in(own, position), (shards_of,), jnp.float32, least / len(split), largest / len(split)))
        level = level * jnp.repeat(steps, dims[position] // shards_of).reshape([-1 if axis == position else 1 for axis in range(len(dims))])
    return level


def gaussian(stream_key, dims, width, reach, pieces=(), kind=jnp.bfloat16):
    result = jax.random.normal(stream_key, dims, jnp.float32) * width
    if len(pieces) > 0:
        result = block_levels(stream_key, dims, pieces, -0.22, 0.18) * result
    return jnp.clip(result, min=-reach, max=reach).astype(kind)


def setup_inputs(seed: int = 0) -> dict:
    seeds = jax.random.split(jax.random.key(seed), 8)
    return {
        "inputs": gaussian(seeds[0], (TOKENS, D), 0.125, 1.0, ((0, 32),)),
        "up_codes": draw_up_codes(jax.random.fold_in(seeds[7], 71), 0),
        "up_scales": jnp.clip(jnp.exp(math.log(0.0008) - 2.3025851 * jax.random.uniform(seeds[2], (D // GROUP, F), jnp.float32) ** block_levels(seeds[2], (D // GROUP, F), ((0, 32), (1, 8)), -0.2, 0.2)), 7.999999797903001e-05, 0.0008),
        "gate_codes": draw_gate_codes(jax.random.fold_in(seeds[7], 71), 0),
        "gate_scales": jnp.clip(jnp.exp(math.log(0.0008) - 2.3025851 * jax.random.uniform(seeds[4], (D // GROUP, F), jnp.float32) ** block_levels(seeds[4], (D // GROUP, F), ((0, 32), (1, 8)), -0.2, 0.2)), 7.999999797903001e-05, 0.0008),
        "grad_up": gaussian(seeds[5], (TOKENS, F), 0.125, 1.0, ((0, 32), (1, 8))),
        "grad_gate": gaussian(seeds[6], (TOKENS, F), 0.125, 1.0, ((0, 32), (1, 8))),
    }


def dequant(codes, scales):
    return (codes.astype(jnp.float32) * jnp.repeat(scales, GROUP, axis=0)).astype(jnp.bfloat16)

def scale_grad(hat, codes):
    prod = (hat * codes.astype(jnp.float32)).reshape(D // GROUP, GROUP, F)
    return lax.optimization_barrier(jnp.sum(prod, axis=1)) / jnp.sqrt(jnp.float32(GROUP * 127))

def reference(inputs, up_codes, up_scales, gate_codes, gate_scales, grad_up, grad_gate):
    w_up = dequant(up_codes, up_scales)
    w_gate = dequant(gate_codes, gate_scales)
    block = F // N_COL
    total = jnp.zeros((TOKENS, D), jnp.float32)
    for index in range(N_COL):
        lo = index * block
        part = jnp.dot(grad_up[:, lo:lo + block], w_up[:, lo:lo + block].T, preferred_element_type=jnp.float32)
        part = part + jnp.dot(grad_gate[:, lo:lo + block], w_gate[:, lo:lo + block].T, preferred_element_type=jnp.float32)
        total = total + lax.optimization_barrier(part.astype(jnp.bfloat16)).astype(jnp.float32)
    input_grad = total.astype(jnp.bfloat16)
    up_hat = jnp.dot(inputs.T, grad_up, preferred_element_type=jnp.float32)
    gate_hat = jnp.dot(inputs.T, grad_gate, preferred_element_type=jnp.float32)
    up_keep = (up_codes > -128) & (up_codes < 127)
    gate_keep = (gate_codes > -128) & (gate_codes < 127)
    up_weight_grad = jnp.where(up_keep, up_hat, jnp.float32(0.0))
    gate_weight_grad = jnp.where(gate_keep, gate_hat, jnp.float32(0.0))
    return (input_grad, up_weight_grad, gate_weight_grad, scale_grad(up_hat, up_codes), scale_grad(gate_hat, gate_codes))
```

```python
import functools

import jax
import jax.numpy as jnp
from jax import lax
from jax.experimental import pallas as pl
from jax.experimental.pallas import tpu as pltpu
from jax.sharding import PartitionSpec as P

GROUP = 128
NY, NX, NZ = 4, 4, 8
MESH = pl.DeviceIdType.MESH
F32, BF16 = jnp.float32, jnp.bfloat16
HALF = 64

PAIRS = (
    ((-1, 0), (1, 0)),
    ((0, -1), (0, 1)),
    ((0, 0), (2, 0)),
    ((-1, -1), (-1, 1)),
    ((1, -1), (1, 1)),
    ((2, -1), (2, 1)),
    ((0, 2), (-1, 2)),
    ((1, 2), (2, 2)),
)
PLACE = {piece: (p, s) for p, pair in enumerate(PAIRS) for s, piece in enumerate(pair)}
FULL = [(o1, o2) for o2 in (0, -1, 1) for o1 in (-1, 1, 0, 2) if o2 or abs(o1) == 1]
HALVES = [(2, 0), (0, 2), (-1, 2), (1, 2), (2, 2)]
SEM = {(piece, None): i for i, piece in enumerate(FULL)}
for piece in HALVES:
    for part in (0, 1):
        SEM[(piece, part)] = len(SEM)
N_SEM = len(SEM)


def wrap(o):
    return 2 if o in (2, -2) else o


def dot(a, b, ca, cb):
    return lax.dot_general(a, b, (((ca,), (cb,)), ((), ())), preferred_element_type=F32)


def pick(index, table):
    out = jnp.int32(table[0])
    for k in range(1, len(table)):
        out = jnp.where(index == k, jnp.int32(table[k]), out)
    return out


def kernel(
    inputs, up_codes, up_scales, gate_codes, gate_scales, grad_up, grad_gate,
    out_grad, out_up, out_gate, out_up_scale, out_gate_scale,
    g, slab, codes, w, acc, other_hat, own, to_sib, from_sib, to_z, from_z, scales, scale_out,
    g_send, g_recv, own_sem, code_sem, a_send, a_recv, r_send, r_recv,
    s_send, s_recv, w_send, w_recv, x_send, x_recv, z_send, z_recv, h_send, h_recv, o_sem,
):
    row, z = lax.axis_index("row"), lax.axis_index("col")
    c = lax.rem(row, 2)
    chip = row // 2
    y, x = chip // NX, lax.rem(chip, NX)
    sibling = (row + 1 - 2 * c, z)

    def at(dy, dx):
        return (((y + dy + NY) % NY * NX + (x + dx + NX) % NX) * 2 + c, z)

    def along(h, axis, o):
        return at(0, o) if (h == 0) == (axis == 0) else at(o, 0)

    def at_z(k):
        return (row, (z + k + NZ) % NZ)

    def remote(src, dst, send, recv, device):
        return pltpu.make_async_remote_copy(
            src_ref=src, dst_ref=dst, send_sem=send, recv_sem=recv,
            device_id=device, device_id_type=MESH,
        )

    barrier = pltpu.get_barrier_semaphore()
    partners = [at(dy, dx) for dy in range(NY) for dx in range(NX) if dy or dx]
    partners += [sibling] + [at_z(k) for k in range(1, NZ)]
    for device in partners:
        pl.semaphore_signal(barrier, inc=1, device_id=device, device_id_type=MESH)
    code_copies = [
        pltpu.make_async_copy(src, codes.at[i], code_sem.at[i])
        for i, src in enumerate((up_codes, gate_codes))
    ]
    for copy in code_copies:
        copy.start()
    p0, s0 = PLACE[(0, 0)]

    def start_own(keep):
        pltpu.make_async_copy(keep, g.at[p0, c, s0], own_sem.at[0]).start()

    def start_give(give):
        remote(give, g.at[p0, c, s0], own_sem.at[1], own_sem.at[2], sibling).start()

    pl.when(c == 0)(lambda: start_own(grad_up))
    pl.when(c == 1)(lambda: start_own(grad_gate))
    scales[0] = up_scales[...]
    scales[1] = gate_scales[...]
    pl.semaphore_wait(barrier, len(partners))

    pl.when(c == 0)(lambda: start_give(grad_gate))
    pl.when(c == 1)(lambda: start_give(grad_up))

    def a_slot(dy, dx):
        at0, at1 = PLACE[(wrap(dx), wrap(dy))], PLACE[(wrap(dy), wrap(dx))]
        return [jnp.where(c == 0, at0[i], at1[i]) for i in (0, 1)]

    rows_z = pl.ds(pl.multiple_of(z * 16, 16), 16)

    def a_src(dy, dx):
        j = (y + dy + NY) % NY * NX + (x + dx + NX) % NX
        return inputs.at[rows_z, pl.ds(pl.multiple_of(j * 512, 512), 512)]

    offsets = [(dy, dx) for dy in (0, 1, -1, 2) for dx in (0, 1, -1, 2) if dy or dx]
    a_copies = []
    for i, (dy, dx) in enumerate(offsets):
        p, s = a_slot(-dy, -dx)
        copy = remote(
            a_src(dy, dx), slab.at[p, c, s, rows_z], a_send.at[i], a_recv.at[i], at(dy, dx)
        )
        copy.start()
        a_copies.append(copy)
    a_own = pltpu.make_async_copy(a_src(0, 0), slab.at[p0, c, s0, rows_z], a_send.at[15])
    a_own.start()

    def rows_of(part):
        return pl.ds(0, 128) if part is None else pl.ds(part * HALF, HALF)

    def send_piece(h, piece, axis, step, part=None):
        o1, o2 = piece
        there = (wrap(o1 - step), o2) if axis == 0 else (o1, wrap(o2 - step))
        p, s = PLACE[piece]
        q, t = PLACE[there]
        k = SEM[(there, part)]
        rows = rows_of(part)
        remote(
            g.at[p, h, s, rows], g.at[q, h, t, rows], g_send.at[h, k], g_recv.at[h, k],
            along(h, axis, step),
        ).start()

    def piece_copy(h, piece, part=None):
        p, s = PLACE[piece]
        k = SEM[(piece, part)]
        ref = g.at[p, h, s, rows_of(part)]
        return remote(ref, ref, g_send.at[h, k], g_recv.at[h, k], sibling)

    def arrive(h, piece):
        for part in (0, 1) if piece in HALVES else (None,):
            piece_copy(h, piece, part).wait_recv()

    own_piece = g.at[p0, c, s0]
    pltpu.make_async_copy(own_piece, own_piece, own_sem.at[0]).wait()
    sib_piece = g.at[p0, 1 - c, s0]
    remote(sib_piece, sib_piece, own_sem.at[1], own_sem.at[2], sibling).wait_recv()
    for axis in (0, 1):
        for h in (0, 1):
            for step in (1, -1):
                send_piece(h, (0, 0), axis, step)

    for copy in code_copies:
        copy.wait()

    def dequant(matrix, dst):
        def body(i, _):
            r = pl.ds(pl.multiple_of(i * 32, 32), 32)
            scale = scales[matrix, pl.ds(i // 4, 1), :]
            dst[r, :] = (codes[matrix, r, :].astype(F32) * scale).astype(BF16)
            return 0

        lax.fori_loop(0, 8, body, 0)

    dequant(1 - c, w.at[2])
    w_copy = remote(w.at[2], w.at[c], w_send, w_recv, sibling)
    w_copy.start()
    dequant(c, w.at[c])
    acc[...] = jnp.zeros_like(acc)

    def block(k, half=None):
        zb = (z + k + 2 * NZ) % NZ
        r = pl.ds(pl.multiple_of(zb * 16, 16), 16)
        pairs = pl.ds(0, 8) if half is None else pl.ds(half * 4, 4)
        return slab.at[pairs, c, :, r, :], zb

    def ring_copy(k, step, half=None):
        ref, _ = block(k, half)
        i = abs(k) + (0 if step == 1 else 4)
        return remote(ref, ref, r_send.at[i], r_recv.at[i], at_z(step))

    def to_sibling(k, half=None):
        ref, _ = block(k, half)
        i = k + 3 if half is None else 7 + half
        return remote(ref, ref, s_send.at[i], s_recv.at[i], sibling)

    def ring_arrive(k, step, half=None):
        ref, _ = block(k - step, half)
        i = abs(k) + (0 if step == 1 else 4)
        remote(ref, ref, r_send.at[i], r_recv.at[i], at_z(step)).wait_recv()

    a_own.wait()
    for copy in a_copies:
        copy.wait_recv()
    ring_copy(0, 1).start()
    ring_copy(0, -1).start()
    to_sibling(0).start()

    def ring_step(k):
        ring_arrive(-(k - 1), 1)
        ring_copy(-k, 1, 0 if k == 3 else None).start()
        to_sibling(-k).start()
        ring_arrive(k - 1, -1)
        ring_copy(k, -1, 1 if k == 3 else None).start()
        to_sibling(k).start()

    def ring_end():
        ring_arrive(-3, 1, 0)
        to_sibling(-4, 0).start()
        ring_arrive(3, -1, 1)
        to_sibling(4, 1).start()

    def sibling_slab(k, half=None):
        zb = (z + k + 2 * NZ) % NZ
        r = pl.ds(pl.multiple_of(zb * 16, 16), 16)
        pairs = pl.ds(0, 8) if half is None else pl.ds(half * 4, 4)
        ref = slab.at[pairs, 1 - c, :, r, :]
        i = k + 3 if half is None else 7 + half
        return remote(ref, ref, s_send.at[i], s_recv.at[i], sibling)

    ring_step(1)
    remote(w.at[1 - c], w.at[1 - c], w_send, w_recv, sibling).wait_recv()

    def event(pieces):
        for h in (0, 1):
            for piece in pieces:
                arrive(h, piece)
                o1, o2 = piece
                if o2 == 0:
                    if o1 == -1:
                        send_piece(h, piece, 0, 1, 0)
                    if o1 == 1:
                        send_piece(h, piece, 0, -1, 1)
                    send_piece(h, piece, 1, 1)
                    send_piece(h, piece, 1, -1)
                elif o2 == -1:
                    send_piece(h, piece, 1, 1, 0)
                elif o2 == 1:
                    send_piece(h, piece, 1, -1, 1)

    def control(n):
        def when(k, *acts):
            @pl.when(n == k)
            def _():
                for act in acts:
                    act()

        when(0, lambda: event(PAIRS[0]))
        when(2, lambda: ring_step(2), lambda: event(PAIRS[1]))
        when(3, lambda: ring_step(3))

        def slab_all():
            ring_end()
            for k in range(-3, 4):
                sibling_slab(k).wait_recv()
            sibling_slab(-4, 0).wait_recv()
            sibling_slab(4, 1).wait_recv()

        when(4, lambda: event(((2, 0),)), slab_all)
        for p in (3, 4, 5, 6, 7):
            when(2 * p, functools.partial(event, PAIRS[p]))

    def back(n):
        p, h = n // 2, lax.rem(n, 2)
        piece = g[p, h].reshape(256, 1792)
        to_sib[n] = dot(piece, w[1 - c], 1, 1).astype(BF16)
        remote(to_sib.at[n], from_sib.at[n], x_send.at[n], x_recv.at[n], sibling).start()
        own[lax.rem(n, 2)] = dot(piece, w[c], 1, 1)

    def combine(n):
        p, h = n // 2, lax.rem(n, 2)
        remote(to_sib.at[n], from_sib.at[n], x_send.at[n], x_recv.at[n], sibling).wait_recv()
        total = own[lax.rem(n, 2)] + from_sib[n].astype(F32)
        to_z[n] = total.astype(BF16)
        for s in (0, 1):
            o1 = pick(p, [pair[s][0] for pair in PAIRS])
            o2 = pick(p, [pair[s][1] for pair in PAIRS])
            yj = (y + jnp.where(h == 0, o2, o1) + NY) % NY
            xj = (x + jnp.where(h == 0, o1, o2) + NX) % NX
            j = yj * NX + xj
            zd, q = j // 2, lax.rem(j, 2)
            rows = pl.ds(s * 128, 128)

            @pl.when(zd == z)
            def _():
                from_z[z, q, h] = to_z[n, rows, :]

            @pl.when(zd != z)
            def _():
                remote(
                    to_z.at[n, rows], from_z.at[z, q, h], z_send.at[n, s], z_recv.at[z, q, h],
                    (row, zd),
                ).start()

    def hats(n):
        p, h = n // 2, lax.rem(n, 2)
        rows = slab[p, h].reshape(256, 512)
        for t in (0, 896):
            piece = g[p, h, :, :, t : t + 896].reshape(256, 896)
            acc[:, t : t + 896] += dot(rows, piece, 0, 0)

    def hats_end(n):
        return jnp.where(n < 4, 0, jnp.minimum(2 * (n - 3), n + 1))

    def step(n, _):
        control(n)
        back(n)

        @pl.when(n > 0)
        def _():
            combine(n - 1)

        def one(i, _):
            hats(i)
            return 0

        lax.fori_loop(hats_end(n - 1), hats_end(n), one, 0)
        return 0

    lax.fori_loop(0, 16, step, 0)
    combine(15)

    mine = pl.ds(pl.multiple_of(c * 256, 256), 256)
    theirs = pl.ds(pl.multiple_of(256 - c * 256, 256), 256)
    h_copy = remote(acc.at[theirs], other_hat, h_send, h_recv, sibling)
    h_copy.start()

    def finish(matrix, ref):
        for group in (0, 1):
            def body(i, total):
                r = pl.ds(pl.multiple_of(group * GROUP + i * 16, 16), 16)
                hat = ref[r, :]
                code = codes[matrix, r, :]
                ref[r, :] = jnp.where((code > -128) & (code < 127), hat, 0.0)
                prod = hat * code.astype(F32)
                return total + prod[:8] + prod[8:]

            total = lax.fori_loop(0, 8, body, jnp.zeros((8, 1792), F32))
            total = jnp.sum(total, axis=0, keepdims=True)
            scale_out[matrix, group : group + 1, :] = total / jnp.sqrt(F32(GROUP * 127))

    finish(c, acc.at[mine])
    acc_mine = acc.at[mine]

    @pl.when(c == 0)
    def _():
        pltpu.make_async_copy(acc_mine, out_up, o_sem.at[0]).start()

    @pl.when(c == 1)
    def _():
        pltpu.make_async_copy(acc_mine, out_gate, o_sem.at[0]).start()

    h_copy.wait()
    finish(1 - c, other_hat)

    @pl.when(c == 0)
    def _():
        pltpu.make_async_copy(other_hat, out_gate, o_sem.at[1]).start()

    @pl.when(c == 1)
    def _():
        pltpu.make_async_copy(other_hat, out_up, o_sem.at[1]).start()

    out_up_scale[...] = scale_out[0]
    out_gate_scale[...] = scale_out[1]

    remote(own_piece, own_piece, own_sem.at[1], own_sem.at[2], sibling).wait_send()
    for copy in a_copies:
        copy.wait_send()
    w_copy.wait_send()
    for h in (0, 1):
        for (piece, part) in SEM:
            piece_copy(h, piece, part).wait_send()
    for k in (0, 1, 2, 3):
        ring_copy(-k, 1, 0 if k == 3 else None).wait_send()
        ring_copy(k, -1, 1 if k == 3 else None).wait_send()
    for k in range(-3, 4):
        to_sibling(k).wait_send()
    to_sibling(-4, 0).wait_send()
    to_sibling(4, 1).wait_send()

    def sent(n, _):
        remote(to_sib.at[n], from_sib.at[n], x_send.at[n], x_recv.at[n], sibling).wait_send()
        p, h = n // 2, lax.rem(n, 2)
        for s in (0, 1):
            o1 = pick(p, [pair[s][0] for pair in PAIRS])
            o2 = pick(p, [pair[s][1] for pair in PAIRS])
            yj = (y + jnp.where(h == 0, o2, o1) + NY) % NY
            xj = (x + jnp.where(h == 0, o1, o2) + NX) % NX
            j = yj * NX + xj

            @pl.when(j // 2 != z)
            def _():
                ref = to_z.at[n, pl.ds(s * 128, 128)]
                remote(ref, ref, z_send.at[n, s], z_recv.at[0, 0, 0], sibling).wait_send()
        return 0

    lax.fori_loop(0, 16, sent, 0)

    def received(k, _):
        zs = lax.rem(z + k, NZ)
        for q in (0, 1):
            for h in (0, 1):
                ref = from_z.at[zs, q, h]
                remote(ref, ref, z_send.at[0, 0], z_recv.at[zs, q, h], sibling).wait_recv()
        return 0

    lax.fori_loop(1, NZ, received, 0)
    for q in (0, 1):
        for h in (0, 1):
            total = from_z[0, q, h].astype(F32)
            for k in range(1, NZ):
                total = total + from_z[k, q, h].astype(F32)
            r = (2 * q + h) * 128
            out_grad[r : r + 128, :] = total.astype(BF16)

    final = pltpu.make_async_copy(acc_mine, out_up, o_sem.at[0])
    final.wait()
    pltpu.make_async_copy(other_hat, out_gate, o_sem.at[1]).wait()


def per_device(inputs, up_codes, up_scales, gate_codes, gate_scales, grad_up, grad_gate):
    vmem = pl.BlockSpec(memory_space=pltpu.VMEM)
    hbm = pl.BlockSpec(memory_space=pl.ANY)
    dma = pltpu.SemaphoreType.DMA
    return pl.pallas_call(
        kernel,
        out_shape=(
            jax.ShapeDtypeStruct((512, 256), BF16),
            jax.ShapeDtypeStruct((256, 1792), F32),
            jax.ShapeDtypeStruct((256, 1792), F32),
            jax.ShapeDtypeStruct((2, 1792), F32),
            jax.ShapeDtypeStruct((2, 1792), F32),
        ),
        in_specs=[hbm, hbm, vmem, hbm, vmem, hbm, hbm],
        out_specs=(vmem, hbm, hbm, vmem, vmem),
        scratch_shapes=[
            pltpu.VMEM((8, 2, 2, 128, 1792), BF16),
            pltpu.VMEM((8, 2, 2, 128, 512), BF16),
            pltpu.VMEM((2, 256, 1792), jnp.int32),
            pltpu.VMEM((3, 256, 1792), BF16),
            pltpu.VMEM((512, 1792), F32),
            pltpu.VMEM((256, 1792), F32),
            pltpu.VMEM((2, 256, 256), F32),
            pltpu.VMEM((16, 256, 256), BF16),
            pltpu.VMEM((16, 256, 256), BF16),
            pltpu.VMEM((16, 256, 256), BF16),
            pltpu.VMEM((NZ, 2, 2, 128, 256), BF16),
            pltpu.VMEM((2, 2, 1792), F32),
            pltpu.VMEM((2, 2, 1792), F32),
            dma((2, N_SEM)), dma((2, N_SEM)),
            dma((3,)),
            dma((2,)),
            dma((16,)), dma((16,)),
            dma((8,)), dma((8,)),
            dma((9,)), dma((9,)),
            dma, dma,
            dma((16,)), dma((16,)),
            dma((16, 2)), dma((NZ, 2, 2)),
            dma, dma,
            dma((2,)),
        ],
        compiler_params=pltpu.CompilerParams(
            collective_id=0, has_side_effects=True, vmem_limit_bytes=56 * 1024 * 1024
        ),
        name="fused_backward",
    )(inputs, up_codes, up_scales, gate_codes, gate_scales, grad_up, grad_gate)


def solution(mesh):
    placed = (
        P("row", None),
        P("row", "col"),
        P("row", "col"),
        P("row", "col"),
        P("row", "col"),
        P("row", "col"),
        P("row", "col"),
    )
    return jax.shard_map(
        per_device,
        mesh=mesh,
        in_specs=placed,
        out_specs=(
            P("col", "row"),
            P("row", "col"),
            P("row", "col"),
            P("row", "col"),
            P("row", "col"),
        ),
        check_vma=False,
    )
```

```python
import functools

import jax
import jax.numpy as jnp
from jax import lax
from jax.experimental import pallas as pl
from jax.experimental.pallas import tpu as pltpu
from jax.sharding import PartitionSpec as P

GROUP = 128
NY, NX, NZ = 4, 4, 8
MESH = pl.DeviceIdType.MESH
F32, BF16 = jnp.float32, jnp.bfloat16
HALF = 64

ORDER = (
    ((0, 0), (-1, 0), (1, 0), (0, -1), (0, 1), (2, 0), (-1, -1), (-1, 1),
     (1, -1), (1, 1), (0, 2), (2, -1), (2, 1), (-1, 2), (1, 2), (2, 2)),
    ((0, 0), (-1, 0), (1, 0), (0, -1), (0, 1), (2, 0), (-1, -1), (-1, 1),
     (2, -1), (2, 1), (0, 2), (1, -1), (1, 1), (-1, 2), (2, 2), (1, 2)),
)
PLACE = [{piece: n for n, piece in enumerate(order)} for order in ORDER]
FULL = [(o1, o2) for o2 in (0, -1, 1) for o1 in (-1, 1, 0, 2) if o2 or abs(o1) == 1]
HALVES = [(2, 0), (0, 2), (-1, 2), (1, 2), (2, 2)]
SEM = {(piece, None): i for i, piece in enumerate(FULL)}
for piece in HALVES:
    for part in (0, 1):
        SEM[(piece, part)] = len(SEM)
N_SEM = len(SEM)


EARLY, SWITCH = 2, 14


def hop_steps():
    table = [{}, {}, {}, {}, {}]
    for n in range(16):
        step = n + 1
        for k in range(5):
            table[k].setdefault(step, []).append(n)
            step += EARLY if step < SWITCH else 1
    return table


HOPS = hop_steps()
LAST_HOP = max(step for table in HOPS for step in table)


def wrap(o):
    return 2 if o in (2, -2) else o


def dot(a, b, ca, cb):
    return lax.dot_general(a, b, (((ca,), (cb,)), ((), ())), preferred_element_type=F32)


def pick(index, table):
    out = jnp.int32(table[0])
    for k in range(1, len(table)):
        out = jnp.where(index == k, jnp.int32(table[k]), out)
    return out


def kernel(
    inputs, up_codes, up_scales, gate_codes, gate_scales, grad_up, grad_gate,
    out_grad, out_up, out_gate, out_up_scale, out_gate_scale,
    g, slab, codes, w, acc, other_hat, own, to_sib, from_sib, to_z, z_in, scales, scale_out,
    g_send, g_recv, own_sem, code_sem, a_send, a_recv, r_send, r_recv,
    s_send, s_recv, w_send, w_recv, x_send, x_recv, z_send, z_recv, h_send, h_recv, o_sem,
):
    row, z = lax.axis_index("row"), lax.axis_index("col")
    c = lax.rem(row, 2)
    chip = row // 2
    y, x = chip // NX, lax.rem(chip, NX)
    sibling = (row + 1 - 2 * c, z)

    def at(dy, dx):
        return (((y + dy + NY) % NY * NX + (x + dx + NX) % NX) * 2 + c, z)

    def along(h, axis, o):
        return at(0, o) if (h == 0) == (axis == 0) else at(o, 0)

    def at_z(k):
        return (row, (z + k + NZ) % NZ)

    def remote(src, dst, send, recv, device):
        return pltpu.make_async_remote_copy(
            src_ref=src, dst_ref=dst, send_sem=send, recv_sem=recv,
            device_id=device, device_id_type=MESH,
        )

    barrier = pltpu.get_barrier_semaphore()
    partners = [at(dy, dx) for dy in range(NY) for dx in range(NX) if dy or dx]
    partners += [sibling, at_z(1), at_z(-1)]
    for device in partners:
        pl.semaphore_signal(barrier, inc=1, device_id=device, device_id_type=MESH)
    code_copies = [
        pltpu.make_async_copy(src, codes.at[i], code_sem.at[i])
        for i, src in enumerate((up_codes, gate_codes))
    ]
    code_copies += [
        pltpu.make_async_copy(src, scales.at[i], code_sem.at[2 + i])
        for i, src in enumerate((up_scales, gate_scales))
    ]
    for copy in code_copies:
        copy.start()

    def start_own(keep):
        pltpu.make_async_copy(keep, g.at[0, c], own_sem.at[0]).start()

    def start_give(give):
        remote(give, g.at[0, c], own_sem.at[1], own_sem.at[2], sibling).start()

    pl.when(c == 0)(lambda: start_own(grad_up))
    pl.when(c == 1)(lambda: start_own(grad_gate))
    pl.semaphore_wait(barrier, len(partners))

    pl.when(c == 0)(lambda: start_give(grad_gate))
    pl.when(c == 1)(lambda: start_give(grad_up))

    def rows_of(part):
        return pl.ds(0, 128) if part is None else pl.ds(part * HALF, HALF)

    def send_piece(h, piece, axis, step, part=None):
        o1, o2 = piece
        there = (wrap(o1 - step), o2) if axis == 0 else (o1, wrap(o2 - step))
        n, m = PLACE[h][piece], PLACE[h][there]
        k = SEM[(there, part)]
        rows = rows_of(part)
        remote(
            g.at[n, h, rows], g.at[m, h, rows], g_send.at[h, k], g_recv.at[h, k],
            along(h, axis, step),
        ).start()

    def piece_copy(h, piece, part=None):
        k = SEM[(piece, part)]
        ref = g.at[PLACE[h][piece], h, rows_of(part)]
        return remote(ref, ref, g_send.at[h, k], g_recv.at[h, k], sibling)

    def arrive(h, piece):
        for part in (0, 1) if piece in HALVES else (None,):
            piece_copy(h, piece, part).wait_recv()

    own_piece = g.at[0, c]
    pltpu.make_async_copy(own_piece, own_piece, own_sem.at[0]).wait()

    def send_own(h):
        for axis in (0, 1):
            for step in (1, -1):
                send_piece(h, (0, 0), axis, step)

    pl.when(c == 0)(lambda: send_own(0))
    pl.when(c == 1)(lambda: send_own(1))

    def a_slot(dy, dx):
        at0, at1 = PLACE[0][(wrap(dx), wrap(dy))], PLACE[1][(wrap(dy), wrap(dx))]
        return jnp.where(c == 0, at0, at1)

    rows_z = pl.ds(pl.multiple_of(z * 16, 16), 16)

    def a_src(dy, dx):
        j = (y + dy + NY) % NY * NX + (x + dx + NX) % NX
        return inputs.at[rows_z, pl.ds(pl.multiple_of(j * 512, 512), 512)]

    offsets = [(dy, dx) for dy in (0, 1, -1, 2) for dx in (0, 1, -1, 2) if dy or dx]
    a_copies = []
    for i, (dy, dx) in enumerate(offsets):
        n = a_slot(-dy, -dx)
        copy = remote(
            a_src(dy, dx), slab.at[n, c, rows_z], a_send.at[i], a_recv.at[i], at(dy, dx)
        )
        copy.start()
        a_copies.append(copy)
    a_own = pltpu.make_async_copy(a_src(0, 0), slab.at[0, c, rows_z], a_send.at[15])
    a_own.start()

    sib_piece = g.at[0, 1 - c]
    remote(sib_piece, sib_piece, own_sem.at[1], own_sem.at[2], sibling).wait_recv()
    pl.when(c == 0)(lambda: send_own(1))
    pl.when(c == 1)(lambda: send_own(0))

    for copy in code_copies:
        copy.wait()

    def dequant(matrix, dst):
        def body(i, _):
            r = pl.ds(pl.multiple_of(i * 32, 32), 32)
            scale = scales[matrix, pl.ds(i // 4, 1), :]
            dst[r, :] = (codes[matrix, r, :].astype(F32) * scale).astype(BF16)
            return 0

        lax.fori_loop(0, 8, body, 0)

    dequant(1 - c, w.at[2])
    w_copy = remote(w.at[2], w.at[c], w_send, w_recv, sibling)
    w_copy.start()
    dequant(c, w.at[c])
    acc[...] = jnp.zeros_like(acc)

    def block(k, half=None):
        zb = (z + k + 2 * NZ) % NZ
        r = pl.ds(pl.multiple_of(zb * 16, 16), 16)
        pairs = pl.ds(0, 16) if half is None else pl.ds(half * 8, 8)
        return slab.at[pairs, c, r, :], zb

    def ring_copy(k, step, half=None):
        ref, _ = block(k, half)
        i = abs(k) + (0 if step == 1 else 4)
        return remote(ref, ref, r_send.at[i], r_recv.at[i], at_z(step))

    def to_sibling(k, half=None):
        ref, _ = block(k, half)
        i = k + 3 if half is None else 7 + half
        return remote(ref, ref, s_send.at[i], s_recv.at[i], sibling)

    def ring_arrive(k, step, half=None):
        ref, _ = block(k - step, half)
        i = abs(k) + (0 if step == 1 else 4)
        remote(ref, ref, r_send.at[i], r_recv.at[i], at_z(step)).wait_recv()

    a_own.wait()
    for copy in a_copies:
        copy.wait_recv()
    ring_copy(0, 1).start()
    ring_copy(0, -1).start()
    to_sibling(0).start()

    def ring_step(k):
        ring_arrive(-(k - 1), 1)
        ring_copy(-k, 1, 0 if k == 3 else None).start()
        to_sibling(-k).start()
        ring_arrive(k - 1, -1)
        ring_copy(k, -1, 1 if k == 3 else None).start()
        to_sibling(k).start()

    def ring_end():
        ring_arrive(-3, 1, 0)
        to_sibling(-4, 0).start()
        ring_arrive(3, -1, 1)
        to_sibling(4, 1).start()

    def sibling_slab(k, half=None):
        zb = (z + k + 2 * NZ) % NZ
        r = pl.ds(pl.multiple_of(zb * 16, 16), 16)
        pairs = pl.ds(0, 16) if half is None else pl.ds(half * 8, 8)
        ref = slab.at[pairs, 1 - c, r, :]
        i = k + 3 if half is None else 7 + half
        return remote(ref, ref, s_send.at[i], s_recv.at[i], sibling)

    ring_step(1)
    remote(w.at[1 - c], w.at[1 - c], w_send, w_recv, sibling).wait_recv()

    def forward(h, piece):
        o1, o2 = piece
        if o2 == 0 and o1:
            if o1 == -1:
                send_piece(h, piece, 0, 1, 0)
            if o1 == 1:
                send_piece(h, piece, 0, -1, 1)
            if (h, o1) != (1, 1):
                send_piece(h, piece, 1, 1)
                send_piece(h, piece, 1, -1)
            if (h, o1) == (1, 2):
                send_piece(h, (1, 0), 1, 1)
                send_piece(h, (1, 0), 1, -1)
        elif o2 == -1:
            send_piece(h, piece, 1, 1, 0)
        elif o2 == 1:
            send_piece(h, piece, 1, -1, 1)

    def slab_all():
        ring_end()
        for k in range(-3, 4):
            sibling_slab(k).wait_recv()
        sibling_slab(-4, 0).wait_recv()
        sibling_slab(4, 1).wait_recv()

    def control(n):
        def when(k, *acts):
            @pl.when(n == k)
            def _():
                for act in acts:
                    act()

        def item(k):
            for h in (0, 1):
                arrive(h, ORDER[h][k])
                forward(h, ORDER[h][k])

        for k in range(1, 16):
            if k in (1, 3, 6, 8, 11):
                when(k, functools.partial(item, k), functools.partial(item, k + 1))
            elif k not in (2, 4, 7, 9, 12):
                when(k, functools.partial(item, k))
        when(3, lambda: ring_step(2))
        when(4, lambda: ring_step(3))
        when(5, slab_all)

    def back(n):
        piece = g[n].reshape(256, 1792)
        to_sib[n] = dot(piece, w[1 - c], 1, 1).astype(BF16)
        remote(to_sib.at[n], from_sib.at[n], x_send.at[n], x_recv.at[n], sibling).start()
        own[lax.rem(n, 2)] = dot(piece, w[c], 1, 1)

    def owner(n, h):
        o1 = pick(n, [piece[0] for piece in ORDER[h]])
        o2 = pick(n, [piece[1] for piece in ORDER[h]])
        yj, xj = (y + (o1, o2)[1 - h] + NY) % NY, (x + (o1, o2)[h] + NX) % NX
        j = yj * NX + xj
        return (j // 2 - z + NZ) % NZ, lax.rem(j, 2)

    def combine(n):
        remote(to_sib.at[n], from_sib.at[n], x_send.at[n], x_recv.at[n], sibling).wait_recv()
        total = own[lax.rem(n, 2)] + from_sib[n].astype(F32)
        to_z[n] = total.astype(BF16)

    def z_copy(n, h, d, rows):
        return remote(
            to_z.at[n, pl.ds(h * 128 + rows[0], rows[1])], z_in.at[n, h, d, pl.ds(*rows)],
            z_send.at[n, h, d], z_recv.at[n, h, d], at_z(1 - 2 * d),
        )

    def out_rows(q, h):
        return pl.ds(pl.multiple_of((2 * q + h) * 128, 128), 128)

    def hop(n, h, distance):
        delta, q = owner(n, h)
        if distance == 4:
            @pl.when(delta == 4)
            def _():
                z_copy(n, h, 0, (0, HALF)).start()
                z_copy(n, h, 1, (HALF, HALF)).start()
        elif distance:
            d = jnp.where(delta < 4, 0, 1)

            @pl.when((delta == distance) | (delta == NZ - distance))
            def _():
                rows = (d * HALF, HALF) if distance == 3 else (0, 128)
                z_copy(n, h, d, rows).wait_recv()
                here = pl.ds(h * 128 + rows[0], rows[1])
                total = to_z[n, here, :].astype(F32) + z_in[n, h, d, pl.ds(*rows), :].astype(F32)
                to_z[n, here, :] = total.astype(BF16)
                z_copy(n, h, d, (0, 128)).start()
        else:
            @pl.when(delta == 0)
            def _():
                total = to_z[n, pl.ds(h * 128, 128), :].astype(F32)
                for d in (0, 1):
                    z_copy(n, h, d, (0, 128)).wait_recv()
                    total = total + z_in[n, h, d].astype(F32)
                out_grad[out_rows(q, h), :] = total.astype(BF16)

    def hops(n):
        for k in range(5):
            for slot in range(max(len(items) for items in HOPS[k].values())):
                items = [(HOPS[k].get(t, []) + [-1, -1, -1])[slot] for t in range(16)]
                if max(items) < 0:
                    continue
                m = pick(n, items)

                @pl.when(m >= 0)
                def _():
                    for h in (0, 1):
                        hop(m, h, 4 - k)

    def late_hops(step):
        for k in range(5):
            for m in HOPS[k].get(step, []):
                for h in (0, 1):
                    hop(jnp.int32(m), h, 4 - k)

    def hats(n):
        rows = slab[n].reshape(256, 512)
        for t in (0, 896):
            piece = g[n, :, :, t : t + 896].reshape(256, 896)
            acc[:, t : t + 896] += dot(rows, piece, 0, 0)

    def early_sends():
        remote(own_piece, own_piece, own_sem.at[1], own_sem.at[2], sibling).wait_send()
        for copy in a_copies:
            copy.wait_send()
        w_copy.wait_send()
        for k in (0, 1, 2, 3):
            ring_copy(-k, 1, 0 if k == 3 else None).wait_send()
            ring_copy(k, -1, 1 if k == 3 else None).wait_send()
        for k in range(-3, 4):
            to_sibling(k).wait_send()
        to_sibling(-4, 0).wait_send()
        to_sibling(4, 1).wait_send()

    def hats_end(n):
        return jnp.where(n < 5, 0, jnp.minimum(2 * (n - 4), n + 1))

    def step(n, _):

        control(n)
        back(n)
        pl.when(n > 0)(lambda: combine(n - 1))
        hops(n)

        def one(i, _):
            hats(i)
            return 0

        lax.fori_loop(hats_end(n - 1), hats_end(n), one, 0)
        pl.when(n == 12)(early_sends)
        return 0

    lax.fori_loop(0, 16, step, 0)
    combine(15)
    late_hops(16)

    mine = pl.ds(pl.multiple_of(c * 256, 256), 256)
    theirs = pl.ds(pl.multiple_of(256 - c * 256, 256), 256)
    h_copy = remote(acc.at[theirs], other_hat, h_send, h_recv, sibling)
    h_copy.start()

    def finish(matrix, ref):
        for group in (0, 1):
            def body(i, total):
                r = pl.ds(pl.multiple_of(group * GROUP + i * 16, 16), 16)
                hat = ref[r, :]
                code = codes[matrix, r, :]
                ref[r, :] = jnp.where((code > -128) & (code < 127), hat, 0.0)
                prod = hat * code.astype(F32)
                return total + prod[:8] + prod[8:]

            total = lax.fori_loop(0, 8, body, jnp.zeros((8, 1792), F32))
            total = jnp.sum(total, axis=0, keepdims=True)
            scale_out[matrix, group : group + 1, :] = total / jnp.sqrt(F32(GROUP * 127))

    finish(c, acc.at[mine])
    acc_mine = acc.at[mine]

    @pl.when(c == 0)
    def _():
        pltpu.make_async_copy(acc_mine, out_up, o_sem.at[0]).start()

    @pl.when(c == 1)
    def _():
        pltpu.make_async_copy(acc_mine, out_gate, o_sem.at[0]).start()

    late_hops(17)
    h_copy.wait()
    finish(1 - c, other_hat)
    late_hops(18)

    @pl.when(c == 0)
    def _():
        pltpu.make_async_copy(other_hat, out_gate, o_sem.at[1]).start()

    @pl.when(c == 1)
    def _():
        pltpu.make_async_copy(other_hat, out_up, o_sem.at[1]).start()

    out_up_scale[...] = scale_out[0]
    out_gate_scale[...] = scale_out[1]

    def sent(n, _):
        remote(to_sib.at[n], from_sib.at[n], x_send.at[n], x_recv.at[n], sibling).wait_send()
        for h in (0, 1):
            delta, _ = owner(n, h)

            @pl.when(delta == 4)
            def _():
                z_copy(n, h, 0, (0, HALF)).wait_send()
                z_copy(n, h, 1, (HALF, HALF)).wait_send()

            @pl.when((delta != 0) & (delta != 4))
            def _():
                z_copy(n, h, jnp.where(delta < 4, 0, 1), (0, 128)).wait_send()
        return 0

    for h in (0, 1):
        for piece, part in SEM:
            piece_copy(h, piece, part).wait_send()
    late_hops(19)
    lax.fori_loop(0, 14, sent, 0)
    for last in range(20, LAST_HOP + 1):
        late_hops(last)
    lax.fori_loop(14, 16, sent, 0)
    final = pltpu.make_async_copy(acc_mine, out_up, o_sem.at[0])
    final.wait()
    pltpu.make_async_copy(other_hat, out_gate, o_sem.at[1]).wait()


def emit(*refs):
    sources, results, sems = refs[:5], refs[5:10], refs[10]
    copies = [
        pltpu.make_async_copy(a, b, sems.at[i]) for i, (a, b) in enumerate(zip(sources, results))
    ]
    for copy in copies:
        copy.start()
    for copy in copies:
        copy.wait()


def per_device(inputs, up_codes, up_scales, gate_codes, gate_scales, grad_up, grad_gate):
    vmem = pl.BlockSpec(memory_space=pltpu.VMEM)
    hbm = pl.BlockSpec(memory_space=pltpu.HBM)
    anywhere = pl.BlockSpec(memory_space=pl.ANY)
    dma = pltpu.SemaphoreType.DMA
    pinned = [
        pltpu.with_memory_space_constraint(a, pltpu.HBM)
        for a in (inputs, up_codes, up_scales, gate_codes, gate_scales, grad_up, grad_gate)
    ]
    results = pl.pallas_call(
        kernel,
        out_shape=(
            jax.ShapeDtypeStruct((512, 256), BF16),
            jax.ShapeDtypeStruct((256, 1792), F32),
            jax.ShapeDtypeStruct((256, 1792), F32),
            jax.ShapeDtypeStruct((2, 1792), F32),
            jax.ShapeDtypeStruct((2, 1792), F32),
        ),
        in_specs=[hbm] * 7,
        out_specs=(vmem, anywhere, anywhere, vmem, vmem),
        scratch_shapes=[
            pltpu.VMEM((16, 2, 128, 1792), BF16),
            pltpu.VMEM((16, 2, 128, 512), BF16),
            pltpu.VMEM((2, 256, 1792), jnp.int32),
            pltpu.VMEM((3, 256, 1792), BF16),
            pltpu.VMEM((512, 1792), F32),
            pltpu.VMEM((256, 1792), F32),
            pltpu.VMEM((2, 256, 256), F32),
            pltpu.VMEM((16, 256, 256), BF16),
            pltpu.VMEM((16, 256, 256), BF16),
            pltpu.VMEM((16, 256, 256), BF16),
            pltpu.VMEM((16, 2, 2, 128, 256), BF16),
            pltpu.VMEM((2, 2, 1792), F32),
            pltpu.VMEM((2, 2, 1792), F32),
            dma((2, N_SEM)), dma((2, N_SEM)),
            dma((3,)),
            dma((4,)),
            dma((16,)), dma((16,)),
            dma((8,)), dma((8,)),
            dma((9,)), dma((9,)),
            dma, dma,
            dma((16,)), dma((16,)),
            dma((16, 2, 2)), dma((16, 2, 2)),
            dma, dma,
            dma((2,)),
        ],
        compiler_params=pltpu.CompilerParams(
            collective_id=0, has_side_effects=True, vmem_limit_bytes=48 * 1024 * 1024
        ),
        name="fused_backward",
    )(*pinned)
    return tuple(
        pl.pallas_call(
            emit,
            out_shape=tuple(jax.ShapeDtypeStruct(r.shape, r.dtype) for r in results),
            in_specs=[anywhere] * 5,
            out_specs=(hbm,) * 5,
            scratch_shapes=[dma((5,))],
            compiler_params=pltpu.CompilerParams(vmem_limit_bytes=1024 * 1024),
            name="emit",
        )(*results)
    )


def solution(mesh):
    placed = (
        P("row", None),
        P("row", "col"),
        P("row", "col"),
        P("row", "col"),
        P("row", "col"),
        P("row", "col"),
        P("row", "col"),
    )
    return jax.shard_map(
        per_device,
        mesh=mesh,
        in_specs=placed,
        out_specs=(
            P("col", "row"),
            P("row", "col"),
            P("row", "col"),
            P("row", "col"),
            P("row", "col"),
        ),
        check_vma=False,
    )
```

```python
import functools

import jax
import jax.numpy as jnp
from jax import lax
from jax.experimental import pallas as pl
from jax.experimental.pallas import tpu as pltpu
from jax.sharding import PartitionSpec as P

GROUP = 128
NY, NX, NZ = 4, 4, 8
MESH = pl.DeviceIdType.MESH
F32, BF16 = jnp.float32, jnp.bfloat16
HALF = 64

ORDER = (
    ((0, 0), (-1, 0), (1, 0), (0, -1), (0, 1), (2, 0), (-1, -1), (-1, 1),
     (1, -1), (1, 1), (0, 2), (2, -1), (2, 1), (-1, 2), (1, 2), (2, 2)),
    ((0, 0), (-1, 0), (1, 0), (0, -1), (0, 1), (2, 0), (-1, -1), (-1, 1),
     (2, -1), (2, 1), (0, 2), (1, -1), (1, 1), (-1, 2), (2, 2), (1, 2)),
)
PLACE = [{piece: n for n, piece in enumerate(order)} for order in ORDER]
PACKED = [
    sum((o % 4) * 4 ** i for i, o in enumerate(ORDER[0][n] + ORDER[1][n])) for n in range(16)
]
FULL = [(o1, o2) for o2 in (0, -1, 1) for o1 in (-1, 1, 0, 2) if o2 or abs(o1) == 1]
HALVES = [(2, 0), (0, 2), (-1, 2), (1, 2), (2, 2)]
SEM = {(piece, None): i for i, piece in enumerate(FULL)}
for piece in HALVES:
    for part in (0, 1):
        SEM[(piece, part)] = len(SEM)
N_SEM = len(SEM)


EARLY, SWITCH = 2, 14


def hop_steps():
    table = [{}, {}, {}, {}, {}]
    for n in range(16):
        step = n + 1
        for k in range(5):
            table[k].setdefault(step, []).append(n)
            step += EARLY if step < SWITCH else 1
    return table


HOPS = hop_steps()
LAST_HOP = max(step for table in HOPS for step in table)


def wrap(o):
    return 2 if o in (2, -2) else o


def dot(a, b, ca, cb):
    return lax.dot_general(a, b, (((ca,), (cb,)), ((), ())), preferred_element_type=F32)


def pick(index, table):
    out = jnp.int32(table[0])
    for k in range(1, len(table)):
        out = jnp.where(index == k, jnp.int32(table[k]), out)
    return out


def kernel(
    inputs, up_codes, up_scales, gate_codes, gate_scales, grad_up, grad_gate,
    out_grad, out_up, out_gate, out_up_scale, out_gate_scale,
    g, slab, codes, w, acc, other_hat, own, to_sib, from_sib, to_z, z_in, scales, scale_out,
    g_send, g_recv, own_sem, code_sem, a_send, a_recv, r_send, r_recv,
    s_send, s_recv, w_send, w_recv, x_send, x_recv, z_send, z_recv, h_send, h_recv, o_sem,
):
    row, z = lax.axis_index("row"), lax.axis_index("col")
    c = lax.rem(row, 2)
    chip = row // 2
    y, x = chip // NX, lax.rem(chip, NX)
    sibling = (row + 1 - 2 * c, z)

    rem = lambda a, b: lax.rem(a, jnp.int32(b))

    def at(dy, dx):
        return ((rem(y + dy + NY, NY) * NX + rem(x + dx + NX, NX)) * 2 + c, z)

    beside = {(dy, dx): at(dy, dx) for dy, dx in ((0, 1), (0, -1), (1, 0), (-1, 0))}

    def along(h, axis, o):
        return beside[(0, o) if (h == 0) == (axis == 0) else (o, 0)]

    def at_z(k):
        return (row, (z + k + NZ) % NZ)

    def remote(src, dst, send, recv, device):
        return pltpu.make_async_remote_copy(
            src_ref=src, dst_ref=dst, send_sem=send, recv_sem=recv,
            device_id=device, device_id_type=MESH,
        )

    barrier = pltpu.get_barrier_semaphore()
    partners = [at(dy, dx) for dy in range(NY) for dx in range(NX) if dy or dx]
    partners += [sibling, at_z(1), at_z(-1)]
    for device in partners:
        pl.semaphore_signal(barrier, inc=1, device_id=device, device_id_type=MESH)
    code_copies = [
        pltpu.make_async_copy(src, codes.at[i], code_sem.at[i])
        for i, src in enumerate((up_codes, gate_codes))
    ]
    code_copies += [
        pltpu.make_async_copy(src, scales.at[i], code_sem.at[2 + i])
        for i, src in enumerate((up_scales, gate_scales))
    ]
    for copy in code_copies:
        copy.start()

    def start_own(keep):
        pltpu.make_async_copy(keep, g.at[0, c], own_sem.at[0]).start()

    def start_give(give):
        remote(give, g.at[0, c], own_sem.at[1], own_sem.at[2], sibling).start()

    pl.when(c == 0)(lambda: start_own(grad_up))
    pl.when(c == 1)(lambda: start_own(grad_gate))
    pl.semaphore_wait(barrier, len(partners))

    pl.when(c == 0)(lambda: start_give(grad_gate))
    pl.when(c == 1)(lambda: start_give(grad_up))

    def rows_of(part):
        return pl.ds(0, 128) if part is None else pl.ds(part * HALF, HALF)

    def send_piece(h, piece, axis, step, part=None):
        o1, o2 = piece
        there = (wrap(o1 - step), o2) if axis == 0 else (o1, wrap(o2 - step))
        n, m = PLACE[h][piece], PLACE[h][there]
        k = SEM[(there, part)]
        rows = rows_of(part)
        remote(
            g.at[n, h, rows], g.at[m, h, rows], g_send.at[h, k], g_recv.at[h, k],
            along(h, axis, step),
        ).start()

    def piece_copy(h, piece, part=None):
        k = SEM[(piece, part)]
        ref = g.at[PLACE[h][piece], h, rows_of(part)]
        return remote(ref, ref, g_send.at[h, k], g_recv.at[h, k], sibling)

    def arrive(h, piece):
        for part in (0, 1) if piece in HALVES else (None,):
            piece_copy(h, piece, part).wait_recv()

    own_piece = g.at[0, c]
    pltpu.make_async_copy(own_piece, own_piece, own_sem.at[0]).wait()

    def send_own(h):
        for axis in (0, 1):
            for step in (1, -1):
                send_piece(h, (0, 0), axis, step)

    pl.when(c == 0)(lambda: send_own(0))
    pl.when(c == 1)(lambda: send_own(1))

    def a_slot(dy, dx):
        at0, at1 = PLACE[0][(wrap(dx), wrap(dy))], PLACE[1][(wrap(dy), wrap(dx))]
        return jnp.where(c == 0, at0, at1)

    rows_z = pl.ds(pl.multiple_of(z * 16, 16), 16)

    def a_src(dy, dx):
        j = (y + dy + NY) % NY * NX + (x + dx + NX) % NX
        return inputs.at[rows_z, pl.ds(pl.multiple_of(j * 512, 512), 512)]

    offsets = [(dy, dx) for dy in (0, 1, -1, 2) for dx in (0, 1, -1, 2) if dy or dx]
    a_copies = []
    for i, (dy, dx) in enumerate(offsets):
        n = a_slot(-dy, -dx)
        copy = remote(
            a_src(dy, dx), slab.at[n, c, rows_z], a_send.at[i], a_recv.at[i], at(dy, dx)
        )
        copy.start()
        a_copies.append(copy)
    a_own = pltpu.make_async_copy(a_src(0, 0), slab.at[0, c, rows_z], a_send.at[15])
    a_own.start()

    sib_piece = g.at[0, 1 - c]
    remote(sib_piece, sib_piece, own_sem.at[1], own_sem.at[2], sibling).wait_recv()
    pl.when(c == 0)(lambda: send_own(1))
    pl.when(c == 1)(lambda: send_own(0))

    for copy in code_copies:
        copy.wait()

    def dequant(matrix, dst):
        def body(i, _):
            r = pl.ds(pl.multiple_of(i * 32, 32), 32)
            scale = scales[matrix, pl.ds(i // 4, 1), :]
            dst[r, :] = (codes[matrix, r, :].astype(F32) * scale).astype(BF16)
            return 0

        lax.fori_loop(0, 8, body, 0)

    dequant(1 - c, w.at[2])
    w_copy = remote(w.at[2], w.at[c], w_send, w_recv, sibling)
    w_copy.start()
    dequant(c, w.at[c])
    acc[...] = jnp.zeros_like(acc)

    def block(k, half=None):
        zb = (z + k + 2 * NZ) % NZ
        r = pl.ds(pl.multiple_of(zb * 16, 16), 16)
        pairs = pl.ds(0, 16) if half is None else pl.ds(half * 8, 8)
        return slab.at[pairs, c, r, :], zb

    def ring_copy(k, step, half=None):
        ref, _ = block(k, half)
        i = abs(k) + (0 if step == 1 else 4)
        return remote(ref, ref, r_send.at[i], r_recv.at[i], at_z(step))

    def to_sibling(k, half=None):
        ref, _ = block(k, half)
        i = k + 3 if half is None else 7 + half
        return remote(ref, ref, s_send.at[i], s_recv.at[i], sibling)

    def ring_arrive(k, step, half=None):
        ref, _ = block(k - step, half)
        i = abs(k) + (0 if step == 1 else 4)
        remote(ref, ref, r_send.at[i], r_recv.at[i], at_z(step)).wait_recv()

    a_own.wait()
    for copy in a_copies:
        copy.wait_recv()
    ring_copy(0, 1).start()
    ring_copy(0, -1).start()
    to_sibling(0).start()

    def ring_step(k):
        ring_arrive(-(k - 1), 1)
        ring_copy(-k, 1, 0 if k == 3 else None).start()
        to_sibling(-k).start()
        ring_arrive(k - 1, -1)
        ring_copy(k, -1, 1 if k == 3 else None).start()
        to_sibling(k).start()

    def ring_end():
        ring_arrive(-3, 1, 0)
        to_sibling(-4, 0).start()
        ring_arrive(3, -1, 1)
        to_sibling(4, 1).start()

    def sibling_slab(k, half=None):
        zb = (z + k + 2 * NZ) % NZ
        r = pl.ds(pl.multiple_of(zb * 16, 16), 16)
        pairs = pl.ds(0, 16) if half is None else pl.ds(half * 8, 8)
        ref = slab.at[pairs, 1 - c, r, :]
        i = k + 3 if half is None else 7 + half
        return remote(ref, ref, s_send.at[i], s_recv.at[i], sibling)

    ring_step(1)
    remote(w.at[1 - c], w.at[1 - c], w_send, w_recv, sibling).wait_recv()

    def forward(h, piece):
        o1, o2 = piece
        if o2 == 0 and o1:
            if o1 == -1:
                send_piece(h, piece, 0, 1, 0)
            if o1 == 1:
                send_piece(h, piece, 0, -1, 1)
            if (h, o1) != (1, 1):
                send_piece(h, piece, 1, 1)
                send_piece(h, piece, 1, -1)
            if (h, o1) == (1, 2):
                send_piece(h, (1, 0), 1, 1)
                send_piece(h, (1, 0), 1, -1)
        elif o2 == -1:
            send_piece(h, piece, 1, 1, 0)
        elif o2 == 1:
            send_piece(h, piece, 1, -1, 1)

    def slab_all():
        ring_end()
        for k in range(-3, 4):
            sibling_slab(k).wait_recv()
        sibling_slab(-4, 0).wait_recv()
        sibling_slab(4, 1).wait_recv()

    def control(n):
        def when(k, *acts):
            @pl.when(n == k)
            def _():
                for act in acts:
                    act()

        def item(k):
            for h in (0, 1):
                arrive(h, ORDER[h][k])
                forward(h, ORDER[h][k])

        for k in range(1, 16):
            if k in (1, 3, 6, 8, 11):
                when(k, functools.partial(item, k), functools.partial(item, k + 1))
            elif k not in (2, 4, 7, 9, 12):
                when(k, functools.partial(item, k))
        when(3, lambda: ring_step(2))
        when(4, lambda: ring_step(3))
        when(5, slab_all)

    def back(n):
        piece = g[n].reshape(256, 1792)
        to_sib[n] = dot(piece, w[1 - c], 1, 1).astype(BF16)
        remote(to_sib.at[n], from_sib.at[n], x_send.at[n], x_recv.at[n], sibling).start()
        own[lax.rem(n, 2)] = dot(piece, w[c], 1, 1)

    def owner(n, h):
        if isinstance(n, int):
            o1, o2 = ORDER[h][n]
        else:
            packed = pick(n, PACKED)
            o1, o2 = rem(packed // (1, 16)[h], 4), rem(packed // (4, 64)[h], 4)
        j = rem(y + (o1, o2)[1 - h] + NY, NY) * NX + rem(x + (o1, o2)[h] + NX, NX)
        return rem(j // 2 - z + NZ, NZ), rem(j, 2)

    def owners(n):
        far, chips = zip(*(owner(n, h) for h in (0, 1)))
        return far[0] + 8 * chips[0] + 16 * far[1] + 128 * chips[1]

    def combine(n):
        remote(to_sib.at[n], from_sib.at[n], x_send.at[n], x_recv.at[n], sibling).wait_recv()
        total = own[lax.rem(n, 2)] + from_sib[n].astype(F32)
        to_z[n] = total.astype(BF16)

    def z_copy(n, h, d, rows):
        return remote(
            to_z.at[n, pl.ds(h * 128 + rows[0], rows[1])], z_in.at[n, h, d, pl.ds(*rows)],
            z_send.at[n, h, d], z_recv.at[n, h, d], at_z(1 - 2 * d),
        )

    def out_rows(q, h):
        return pl.ds(pl.multiple_of((2 * q + h) * 128, 128), 128)

    def hop(n, h, distance, code=None):
        if code is None:
            delta, q = owner(n, h)
        else:
            delta, q = rem(code // (1, 16)[h], NZ), rem(code // (8, 128)[h], 2)
        if distance == 4:
            @pl.when(delta == 4)
            def _():
                z_copy(n, h, 0, (0, HALF)).start()
                z_copy(n, h, 1, (HALF, HALF)).start()
        elif distance:
            d = jnp.where(delta < 4, 0, 1)

            @pl.when((delta == distance) | (delta == NZ - distance))
            def _():
                rows = (d * HALF, HALF) if distance == 3 else (0, 128)
                z_copy(n, h, d, rows).wait_recv()
                here = pl.ds(h * 128 + rows[0], rows[1])
                total = to_z[n, here, :].astype(F32) + z_in[n, h, d, pl.ds(*rows), :].astype(F32)
                to_z[n, here, :] = total.astype(BF16)
                z_copy(n, h, d, (0, 128)).start()
        else:
            @pl.when(delta == 0)
            def _():
                total = to_z[n, pl.ds(h * 128, 128), :].astype(F32)
                for d in (0, 1):
                    z_copy(n, h, d, (0, 128)).wait_recv()
                    total = total + z_in[n, h, d].astype(F32)
                out_grad[out_rows(q, h), :] = total.astype(BF16)

    def hops(n, codes):
        for k in range(5):
            m = n - 1 - EARLY * k

            @pl.when(m >= 0)
            def _():
                for h in (0, 1):
                    hop(m, h, 4 - k, codes[EARLY * k])

        for step in range(SWITCH, 16):
            pl.when(n == step)(functools.partial(late_hops, step, EARLY))

    def late_hops(step, regular=None):
        for k in range(5):
            for m in HOPS[k].get(step, []):
                if regular is None or m != step - 1 - regular * k:
                    for h in (0, 1):
                        hop(m, h, 4 - k)

    def hats(n):
        rows = slab[n].reshape(256, 512)
        for t in (0, 896):
            piece = g[n, :, :, t : t + 896].reshape(256, 896)
            acc[:, t : t + 896] += dot(rows, piece, 0, 0)

    def early_sends():
        remote(own_piece, own_piece, own_sem.at[1], own_sem.at[2], sibling).wait_send()
        for copy in a_copies:
            copy.wait_send()
        w_copy.wait_send()
        for k in (0, 1, 2, 3):
            ring_copy(-k, 1, 0 if k == 3 else None).wait_send()
            ring_copy(k, -1, 1 if k == 3 else None).wait_send()
        for k in range(-3, 4):
            to_sibling(k).wait_send()
        to_sibling(-4, 0).wait_send()
        to_sibling(4, 1).wait_send()

    def hats_end(n):
        return jnp.where(n < 5, 0, jnp.minimum(2 * (n - 4), n + 1))

    def step(n, codes):
        codes = (owners(n - 1),) + codes[:-1]

        control(n)
        back(n)
        pl.when(n > 0)(lambda: combine(n - 1))
        hops(n, codes)

        def one(i, _):
            hats(i)
            return 0

        lax.fori_loop(hats_end(n - 1), hats_end(n), one, 0)
        pl.when(n == 12)(early_sends)
        return codes

    lax.fori_loop(0, 16, step, (jnp.int32(0),) * (4 * EARLY + 1))
    combine(15)
    late_hops(16)

    mine = pl.ds(pl.multiple_of(c * 256, 256), 256)
    theirs = pl.ds(pl.multiple_of(256 - c * 256, 256), 256)
    h_copy = remote(acc.at[theirs], other_hat, h_send, h_recv, sibling)
    h_copy.start()

    def finish(matrix, ref):
        for group in (0, 1):
            def body(i, total):
                r = pl.ds(pl.multiple_of(group * GROUP + i * 16, 16), 16)
                hat = ref[r, :]
                code = codes[matrix, r, :]
                ref[r, :] = jnp.where((code > -128) & (code < 127), hat, 0.0)
                prod = hat * code.astype(F32)
                return total + prod[:8] + prod[8:]

            total = lax.fori_loop(0, 8, body, jnp.zeros((8, 1792), F32))
            total = jnp.sum(total, axis=0, keepdims=True)
            scale_out[matrix, group : group + 1, :] = total / jnp.sqrt(F32(GROUP * 127))

    finish(c, acc.at[mine])
    acc_mine = acc.at[mine]

    @pl.when(c == 0)
    def _():
        pltpu.make_async_copy(acc_mine, out_up, o_sem.at[0]).start()

    @pl.when(c == 1)
    def _():
        pltpu.make_async_copy(acc_mine, out_gate, o_sem.at[0]).start()

    late_hops(17)
    h_copy.wait()
    finish(1 - c, other_hat)
    late_hops(18)

    @pl.when(c == 0)
    def _():
        pltpu.make_async_copy(other_hat, out_gate, o_sem.at[1]).start()

    @pl.when(c == 1)
    def _():
        pltpu.make_async_copy(other_hat, out_up, o_sem.at[1]).start()

    out_up_scale[...] = scale_out[0]
    out_gate_scale[...] = scale_out[1]

    def sent(n):
        remote(to_sib.at[n], from_sib.at[n], x_send.at[n], x_recv.at[n], sibling).wait_send()
        for h in (0, 1):
            delta, _ = owner(n, h)

            @pl.when(delta == 4)
            def _():
                z_copy(n, h, 0, (0, HALF)).wait_send()
                z_copy(n, h, 1, (HALF, HALF)).wait_send()

            @pl.when((delta != 0) & (delta != 4))
            def _():
                z_copy(n, h, jnp.where(delta < 4, 0, 1), (0, 128)).wait_send()

    for h in (0, 1):
        for piece, part in SEM:
            piece_copy(h, piece, part).wait_send()
    late_hops(19)
    for n in range(14):
        sent(n)
    for last in range(20, LAST_HOP + 1):
        late_hops(last)
    for n in (14, 15):
        sent(n)
    final = pltpu.make_async_copy(acc_mine, out_up, o_sem.at[0])
    final.wait()
    pltpu.make_async_copy(other_hat, out_gate, o_sem.at[1]).wait()


def emit(*refs):
    sources, results, sems = refs[:5], refs[5:10], refs[10]
    copies = [
        pltpu.make_async_copy(a, b, sems.at[i]) for i, (a, b) in enumerate(zip(sources, results))
    ]
    for copy in copies:
        copy.start()
    for copy in copies:
        copy.wait()


def per_device(inputs, up_codes, up_scales, gate_codes, gate_scales, grad_up, grad_gate):
    vmem = pl.BlockSpec(memory_space=pltpu.VMEM)
    hbm = pl.BlockSpec(memory_space=pltpu.HBM)
    anywhere = pl.BlockSpec(memory_space=pl.ANY)
    dma = pltpu.SemaphoreType.DMA
    pinned = [
        pltpu.with_memory_space_constraint(a, pltpu.HBM)
        for a in (inputs, up_codes, up_scales, gate_codes, gate_scales, grad_up, grad_gate)
    ]
    results = pl.pallas_call(
        kernel,
        out_shape=(
            jax.ShapeDtypeStruct((512, 256), BF16),
            jax.ShapeDtypeStruct((256, 1792), F32),
            jax.ShapeDtypeStruct((256, 1792), F32),
            jax.ShapeDtypeStruct((2, 1792), F32),
            jax.ShapeDtypeStruct((2, 1792), F32),
        ),
        in_specs=[hbm] * 7,
        out_specs=(vmem, anywhere, anywhere, vmem, vmem),
        scratch_shapes=[
            pltpu.VMEM((16, 2, 128, 1792), BF16),
            pltpu.VMEM((16, 2, 128, 512), BF16),
            pltpu.VMEM((2, 256, 1792), jnp.int32),
            pltpu.VMEM((3, 256, 1792), BF16),
            pltpu.VMEM((512, 1792), F32),
            pltpu.VMEM((256, 1792), F32),
            pltpu.VMEM((2, 256, 256), F32),
            pltpu.VMEM((16, 256, 256), BF16),
            pltpu.VMEM((16, 256, 256), BF16),
            pltpu.VMEM((16, 256, 256), BF16),
            pltpu.VMEM((16, 2, 2, 128, 256), BF16),
            pltpu.VMEM((2, 2, 1792), F32),
            pltpu.VMEM((2, 2, 1792), F32),
            dma((2, N_SEM)), dma((2, N_SEM)),
            dma((3,)),
            dma((4,)),
            dma((16,)), dma((16,)),
            dma((8,)), dma((8,)),
            dma((9,)), dma((9,)),
            dma, dma,
            dma((16,)), dma((16,)),
            dma((16, 2, 2)), dma((16, 2, 2)),
            dma, dma,
            dma((2,)),
        ],
        compiler_params=pltpu.CompilerParams(
            collective_id=0, has_side_effects=True, vmem_limit_bytes=48 * 1024 * 1024
        ),
        name="fused_backward",
    )(*pinned)
    return tuple(
        pl.pallas_call(
            emit,
            out_shape=tuple(jax.ShapeDtypeStruct(r.shape, r.dtype) for r in results),
            in_specs=[anywhere] * 5,
            out_specs=(hbm,) * 5,
            scratch_shapes=[dma((5,))],
            compiler_params=pltpu.CompilerParams(vmem_limit_bytes=1024 * 1024),
            name="emit",
        )(*results)
    )


def solution(mesh):
    placed = (
        P("row", None),
        P("row", "col"),
        P("row", "col"),
        P("row", "col"),
        P("row", "col"),
        P("row", "col"),
        P("row", "col"),
    )
    return jax.shard_map(
        per_device,
        mesh=mesh,
        in_specs=placed,
        out_specs=(
            P("col", "row"),
            P("row", "col"),
            P("row", "col"),
            P("row", "col"),
            P("row", "col"),
        ),
        check_vma=False,
    )
```
